32 devices in a mesh: aa: 4 (over z), col: 2 (over core), pb: 4 (over y, x).
Axes of the slice: x: 2, y: 2, z: 4, core: 2. Of those that a mesh axis runs over, the one named last changes fastest.
Arguments:
- b_ac: bfloat16 [1536, 512, 1024], P('pb', 'aa', 'col'), may hold values from -6 to 6
- b_oc: bfloat16 [1536, 32, 1024], P('pb', None, 'col'), may hold values from -6 to 6
- t1: bfloat16 [32, 512], P(None, 'aa'), may hold values from -0.59765625 to 0.59765625
- f_bd: bfloat16 [1536, 256], P('pb'), may hold values from -0.15625 to 0.15625
- t2: bfloat16 [512, 32768], P('aa', ('col', 'pb')), may hold values from -0.046875 to 0.046875
Outputs:
- residual: float32 [512, 4096], P(('col', 'pb'), 'aa')
The draws below stay inside these ranges and needn't reach their ends.
All inputs are finite; a program needn't handle non-finite values.
Results may differ from the reference program's by a relative error of at most 0.0041.
Values may be sent and summed in bfloat16 or wider, within the bound.
A program may use at most 256 MiB of HBM per device.

```python
import jax
import jax.numpy as jnp
from jax import lax

V = 1024
VA = 512
NAUX = 1536
NOCC = 32
BB = 8
DB = 32
PAIRS = 512
N_AA = 4


def raised(result, key, source, target, shards_of, factor):
    def block_of(axis_at):
        return (jnp.arange(result.shape[axis_at]) // (result.shape[axis_at] // shards_of)).reshape((-1,) + (1,) * (result.ndim - 1 - axis_at))

    near = jax.random.permutation(key, shards_of)[block_of(target)]
    second = (block_of(target) + shards_of // 2) % shards_of
    return jnp.where((block_of(source) == near) | (block_of(source) == second), factor * result, result)


def levels(key, dims, cuts, smallest, high):
    gain = 1.0
    for dim, blocks in cuts:
        draws = jax.random.uniform(jax.random.fold_in(jax.random.fold_in(key, 6), dim), (blocks,), jnp.float32, smallest / len(cuts), high / len(cuts))
        gain = gain * jnp.repeat(jnp.exp(draws), dims[dim] // blocks).reshape((-1,) + (1,) * (len(dims) - 1 - dim))
    return gain


def noise(rng, dims, scale, reach, pieces=(), kind=jnp.bfloat16):
    drawn = scale * jax.random.normal(rng, dims, jnp.float32)
    if pieces:
        drawn = drawn * levels(rng, dims, pieces, -0.22, 0.18)
    return jnp.clip(drawn, -reach, reach).astype(kind)


def gaussian_with(rng, extent, deviation, bound, cuts, heavy, kind=jnp.bfloat16):
    drawn = deviation * jax.random.normal(rng, extent, jnp.float32)
    if cuts:
        drawn = drawn * levels(rng, extent, cuts, -0.22, 0.18)
    return jnp.clip(raised(drawn, jax.random.fold_in(rng, 3), *heavy), -bound, bound).astype(kind)


def setup_inputs(seed: int = 0) -> dict:
    splits = jax.random.split(jax.random.key(seed), 6)
    return {
        "b_ac": noise(splits[0], (NAUX, VA, V), 1.0, 6.0, ((0, 4), (1, 4), (2, 2))),
        "b_oc": noise(splits[1], (NAUX, NOCC, V), 1.0, 6.0, ((0, 4), (2, 2))),
        "t1": noise(splits[2], (NOCC, VA), 0.1, 0.59765625, ((1, 4),)),
        "f_bd": noise(splits[3], (NAUX, BB * DB), NAUX ** -0.5, 0.15625, ((0, 4),)),
        "t2": gaussian_with(splits[4], (PAIRS, V * DB), (V * DB) ** -0.5, 0.046875, ((0, 4), (1, 8)), (1, 0, 8, 2.0)),
    }


def reference(b_ac, b_oc, t1, f_bd, t2):
    width = VA // N_AA
    b_occ = b_oc.astype(jnp.float32)

    def one_block(index):
        offset = (index * width).astype(jnp.int32)
        slab = lax.dynamic_slice_in_dim(b_ac, offset, width, 1).astype(jnp.float32)
        singles = lax.dynamic_slice_in_dim(t1, offset, width, 1).astype(jnp.float32)
        correction = jnp.einsum('ka,qkc->qac', singles, b_occ)
        dressed = (slab - correction).astype(jnp.bfloat16)
        ladder = lax.dot_general(dressed.reshape(NAUX, width * V), f_bd, (((0,), (0,)), ((), ())), preferred_element_type=jnp.float32).astype(jnp.bfloat16)
        ladder = ladder.reshape(width, V, BB, DB).transpose(0, 2, 1, 3).reshape(width * BB, V * DB)
        return lax.dot_general(t2, ladder, (((1,), (1,)), ((), ())), preferred_element_type=jnp.float32)

    blocks = lax.map(one_block, jnp.arange(N_AA, dtype=jnp.int32))
    return blocks.transpose(1, 0, 2).reshape(PAIRS, VA * BB)
```

```python
import jax
import jax.numpy as jnp
from jax import lax
from jax.sharding import PartitionSpec as P

BB = 8
DB = 32
LANES = 128


def shards(b_ac, b_oc, t1, f_bd, t2):
    pairs, width = t2.shape
    c_width = width // DB
    if c_width % LANES or pairs % LANES:
        return narrow_shards(b_ac, b_oc, t1, f_bd, t2)
    amplitudes = t2.reshape(pairs, c_width, DB).transpose(0, 2, 1)
    gathered = lax.all_gather(amplitudes, ("aa", "pb"), axis=0)
    n_aa, n_pb = lax.axis_size("aa"), lax.axis_size("pb")
    gathered = gathered.reshape(n_aa, n_pb, pairs, DB, c_width)
    correction = jnp.einsum("ka,qkc->qac", t1, b_oc, preferred_element_type=jnp.float32)
    dressed = (b_ac - correction).astype(jnp.bfloat16)
    ladder = jnp.einsum("qac,qn->anc", dressed, f_bd, preferred_element_type=jnp.float32)
    ladder = ladder.astype(jnp.bfloat16)
    ladder = ladder.reshape(ladder.shape[0], BB, DB, n_pb, c_width)
    partial_sums = jnp.einsum(
        "xpidc,abdpc->xiab", gathered, ladder, preferred_element_type=jnp.float32
    )
    partial_sums = partial_sums.reshape(n_aa * pairs, -1)
    return lax.psum_scatter(partial_sums, ("col", "pb"), scatter_dimension=0, tiled=True)


def narrow_shards(b_ac, b_oc, t1, f_bd, t2):
    correction = jnp.einsum("ka,qkc->qac", t1, b_oc, preferred_element_type=jnp.float32)
    dressed = (b_ac - correction).astype(jnp.bfloat16)
    regrouped = lax.all_to_all(dressed, "pb", split_axis=2, concat_axis=0, tiled=True)
    a_width = regrouped.shape[1]
    c_width = regrouped.shape[2]
    flat_factors = regrouped.reshape(regrouped.shape[0], a_width * c_width)
    contract_rows = (((0,), (0,)), ((), ()))
    factor_all = lax.all_gather(f_bd, "pb", axis=0, tiled=True)
    ladder = lax.dot_general(
        flat_factors, factor_all, contract_rows, preferred_element_type=jnp.float32
    )
    ladder = ladder.astype(jnp.bfloat16)
    ladder = (
        ladder.reshape(a_width, c_width, BB, DB)
        .transpose(0, 2, 1, 3)
        .reshape(a_width * BB, c_width * DB)
    )
    partial_sums = lax.dot_general(
        lax.all_gather(t2, "aa", axis=0, tiled=True),
        ladder,
        (((1,), (1,)), ((), ())),
        preferred_element_type=jnp.float32,
    )
    return lax.psum_scatter(partial_sums, ("col", "pb"), scatter_dimension=0, tiled=True)


def solution(mesh):
    placed = (
        P("pb", "aa", "col"),
        P("pb", None, "col"),
        P(None, "aa"),
        P("pb", None),
        P("aa", ("col", "pb")),
    )
    return jax.shard_map(
        shards, mesh=mesh, in_specs=placed, out_specs=P(("col", "pb"), "aa"), check_vma=False
    )
```

```python
import functools
import math

import jax
import jax.numpy as jnp
from jax import lax
from jax.experimental import pallas as pl
from jax.sharding import PartitionSpec as P

BB = 8
DB = 32
LANES = 128


def dress_rows(rows, b_ac_ref, b_oc_ref, singles_ref, out_ref):
    singles = singles_ref[...]
    for row in range(rows):
        correction = jnp.dot(singles, b_oc_ref[row], preferred_element_type=jnp.float32)
        slab = b_ac_ref[row].astype(jnp.float32)
        out_ref[row] = (slab - correction).astype(out_ref.dtype)


def dress(b_ac, b_oc, singles):
    depth, a_width, c_width = b_ac.shape
    n_occ = b_oc.shape[1]
    rows = math.gcd(depth, 8)
    return pl.pallas_call(
        functools.partial(dress_rows, rows),
        grid=(depth // rows,),
        in_specs=[
            pl.BlockSpec((rows, a_width, c_width), lambda i: (i, 0, 0)),
            pl.BlockSpec((rows, n_occ, c_width), lambda i: (i, 0, 0)),
            pl.BlockSpec((a_width, n_occ), lambda i: (0, 0)),
        ],
        out_specs=pl.BlockSpec((rows, a_width, c_width), lambda i: (i, 0, 0)),
        out_shape=jax.ShapeDtypeStruct(b_ac.shape, b_ac.dtype),
        cost_estimate=pl.CostEstimate(
            flops=2 * b_ac.size * n_occ,
            bytes_accessed=4 * b_ac.size + 2 * b_oc.size,
            transcendentals=0,
        ),
    )(b_ac, b_oc, singles)


def shards(b_ac, b_oc, t1, f_bd, t2):
    pairs, width = t2.shape
    c_width = width // DB
    if c_width % LANES or pairs % LANES:
        return narrow_shards(b_ac, b_oc, t1, f_bd, t2)
    amplitudes = t2.reshape(pairs, c_width, DB).transpose(0, 2, 1)
    gathered = lax.all_gather(amplitudes, ("aa", "pb"), axis=0)
    n_aa, n_pb = lax.axis_size("aa"), lax.axis_size("pb")
    gathered = gathered.reshape(n_aa, n_pb, pairs, DB, c_width)
    dressed = dress(b_ac, b_oc, t1.T)
    ladder = jnp.einsum("qac,qn->anc", dressed, f_bd, preferred_element_type=jnp.float32)
    ladder = ladder.astype(jnp.bfloat16)
    ladder = ladder.reshape(ladder.shape[0], BB, DB, n_pb, c_width)
    partial_sums = jnp.einsum(
        "xpidc,abdpc->xiab", gathered, ladder, preferred_element_type=jnp.float32
    )
    partial_sums = partial_sums.reshape(n_aa * pairs, -1)
    return lax.psum_scatter(partial_sums, ("col", "pb"), scatter_dimension=0, tiled=True)


def narrow_shards(b_ac, b_oc, t1, f_bd, t2):
    correction = jnp.einsum("ka,qkc->qac", t1, b_oc, preferred_element_type=jnp.float32)
    dressed = (b_ac - correction).astype(jnp.bfloat16)
    regrouped = lax.all_to_all(dressed, "pb", split_axis=2, concat_axis=0, tiled=True)
    a_width = regrouped.shape[1]
    c_width = regrouped.shape[2]
    flat_factors = regrouped.reshape(regrouped.shape[0], a_width * c_width)
    contract_rows = (((0,), (0,)), ((), ()))
    factor_all = lax.all_gather(f_bd, "pb", axis=0, tiled=True)
    ladder = lax.dot_general(
        flat_factors, factor_all, contract_rows, preferred_element_type=jnp.float32
    )
    ladder = ladder.astype(jnp.bfloat16)
    ladder = (
        ladder.reshape(a_width, c_width, BB, DB)
        .transpose(0, 2, 1, 3)
        .reshape(a_width * BB, c_width * DB)
    )
    partial_sums = lax.dot_general(
        lax.all_gather(t2, "aa", axis=0, tiled=True),
        ladder,
        (((1,), (1,)), ((), ())),
        preferred_element_type=jnp.float32,
    )
    return lax.psum_scatter(partial_sums, ("col", "pb"), scatter_dimension=0, tiled=True)


def solution(mesh):
    placed = (
        P("pb", "aa", "col"),
        P("pb", None, "col"),
        P(None, "aa"),
        P("pb", None),
        P("aa", ("col", "pb")),
    )
    return jax.shard_map(
        shards, mesh=mesh, in_specs=placed, out_specs=P(("col", "pb"), "aa"), check_vma=False
    )
```
